32 devices in a mesh: pipe: 4 (over y, core), seq: 8 (over z, x).
Axes of the slice: x: 2, y: 2, z: 4, core: 2. Of those that a mesh axis runs over, the one named last changes fastest.
Arguments:
- queries: bfloat16 [4, 2048, 4096], P('pipe', 'seq'), may hold values from -50 to 50
- keys: bfloat16 [4, 2048, 512], P('pipe', 'seq'), may hold values from -4 to 4
- values: bfloat16 [4, 2048, 512], P('pipe', 'seq'), may hold values from -6 to 6
- out_grad: bfloat16 [4, 2048, 4096], P('pipe', 'seq'), may hold values from -96 to 96
- global_blocks: int32 [4, 32, 2], P('pipe'), may hold values from 0 to 15
- random_blocks: int32 [4, 32, 16, 3], P('pipe'), may hold values from 0 to 15
Outputs:
- query_grad: bfloat16 [4, 2048, 4096], P('pipe', 'seq')
- key_grad: bfloat16 [4, 2048, 512], P('pipe', 'seq')
- value_grad: bfloat16 [4, 2048, 512], P('pipe', 'seq')
- incoming_query: bfloat16 [4, 2048, 4096], P('pipe', 'seq')
- incoming_key: bfloat16 [4, 2048, 512], P('pipe', 'seq')
- incoming_value: bfloat16 [4, 2048, 512], P('pipe', 'seq')
The draws below stay inside these ranges and needn't reach their ends.
All inputs are finite; a program needn't handle non-finite values.
Results may differ from the reference program's by a relative error of at most 0.0086.
Values may be sent and summed in bfloat16 or wider, within the bound.
A program may use at most 256 MiB of HBM per device.

```python
import jax
import jax.numpy as jnp
from jax import lax

HEADS = 32
KV_HEADS = 4
HEAD = 128
BLOCK = 128
NGLOB = 2
NRAND = 3
SECTIONS = 4
SEQ_LEN = 2048
NBLK = 16
GROUP = 8


def paired_draw(key):
    base = jax.random.fold_in(key, 7001)
    key_a = jax.random.fold_in(base, 0)
    key_c = jax.random.fold_in(base, 2)
    key_shape = (SECTIONS, SEQ_LEN, KV_HEADS, HEAD)
    query_shape = (SECTIONS, SEQ_LEN, KV_HEADS, GROUP, HEAD)
    key_vals = jnp.clip(jax.random.normal(key_a, key_shape, jnp.float32), -4.0, 4.0)
    query_vals = jnp.clip(jax.random.normal(key_c, query_shape, jnp.float32), -4.0, 4.0)
    return (query_vals.reshape(SECTIONS, SEQ_LEN, HEADS * HEAD), key_vals.reshape(SECTIONS, SEQ_LEN, KV_HEADS * HEAD))


def draw_queries(key, part):
    return paired_draw(key)[0].astype(jnp.bfloat16)


def draw_keys(key, part):
    return paired_draw(key)[1].astype(jnp.bfloat16)


def with_ends(values, own_key, smallest, high):
    longest = values.shape.index(max(values.shape))
    spots = []
    for shift in (0, 1):
        where = [jax.random.randint(jax.random.fold_in(own_key, axis), (), 0, length) for axis, length in enumerate(values.shape)]
        where[longest] = (where[longest] + shift) % values.shape[longest]
        spots.append(tuple(where))
    return values.at[spots[0]].set(smallest).at[spots[1]].set(high)


def shard_levels(own_key, dims, shards, least, high):
    factor_of = 1.0
    for dim, blocks in shards:
        draws = jax.random.uniform(jax.random.fold_in(jax.random.fold_in(own_key, 6), dim), (blocks,), jnp.float32, least / len(shards), high / len(shards))
        factor_of = factor_of * jnp.repeat(jnp.exp(draws), dims[dim] // blocks).reshape((-1,) + (1,) * (len(dims) - 1 - dim))
    return factor_of


def bell_draw(key, extent, spread, bound, pieces=(), kind=jnp.bfloat16):
    values = jax.random.normal(key, extent, jnp.float32) * spread
    if len(pieces) > 0:
        values = shard_levels(key, extent, pieces, -0.22, 0.18) * values
    return jnp.clip(values, min=-bound, max=bound).astype(kind)


def setup_inputs(seed: int = 0) -> dict:
    key_of = jax.random.split(jax.random.key(seed), 7)
    queries = draw_queries(jax.random.fold_in(key_of[6], 71), 0)
    keys = draw_keys(jax.random.fold_in(key_of[6], 71), 0)
    values = bell_draw(key_of[2], (SECTIONS, SEQ_LEN, KV_HEADS * HEAD), 1.0, 6.0, ((0, 4), (1, 8)))
    out_grad = bell_draw(key_of[3], (SECTIONS, SEQ_LEN, HEADS * HEAD), 16.0, 96.0, ((0, 4), (1, 8)))
    global_blocks = with_ends(jax.random.randint(key_of[4], (SECTIONS, HEADS, NGLOB), 0, NBLK), jax.random.fold_in(key_of[4], 1), 0, NBLK - 1).astype(jnp.int32)
    random_blocks = with_ends(jax.random.randint(key_of[5], (SECTIONS, HEADS, NBLK, NRAND), 0, NBLK), jax.random.fold_in(key_of[5], 1), 0, NBLK - 1).astype(jnp.int32)
    return {"queries": queries, "keys": keys, "values": values, "out_grad": out_grad, "global_blocks": global_blocks, "random_blocks": random_blocks}


def block_lists(global_rows, random_rows, first, count):
    query_block = first + jnp.arange(count, dtype=jnp.int32)
    window = (query_block[:, None] + jnp.arange(-1, 2, dtype=jnp.int32)[None, :]) % NBLK
    heads_here = global_rows.shape[0]
    window = jnp.broadcast_to(window[None], (heads_here, count, 3))
    global_tiles = jnp.broadcast_to(global_rows[:, None, :], (heads_here, count, global_rows.shape[1]))
    random_here = lax.dynamic_slice_in_dim(random_rows, first, count, 1)
    return jnp.concatenate([window, global_tiles, random_here], axis=2).astype(jnp.int32)


def backward_tiles(query_rows, grad_rows, key_source, value_source, tile_index):
    pairs = query_rows.shape[0]
    scale = HEAD ** -0.5
    count = pairs // 4

    def step(totals, inputs):
        query_group, grad_group, index_group = inputs
        flat_index = index_group.reshape(-1)
        key_tiles = key_source[flat_index].reshape(4, -1, HEAD).astype(jnp.float32)
        value_tiles = value_source[flat_index].reshape(4, -1, HEAD).astype(jnp.float32)
        query_wide = query_group.astype(jnp.float32)
        grad_wide = grad_group.astype(jnp.float32)
        scores = jnp.einsum("gqd,gkd->gqk", query_wide, key_tiles) * scale
        shifted = jnp.exp(scores - jnp.max(scores, axis=-1, keepdims=True))
        weights = shifted / jnp.sum(shifted, axis=-1, keepdims=True)
        weights_low = lax.optimization_barrier(weights.astype(jnp.bfloat16)).astype(jnp.float32)
        output = jnp.einsum("gqk,gkd->gqd", weights_low, value_tiles)
        row_dot = jnp.sum(grad_wide * output, axis=-1, keepdims=True)
        grad_weights = jnp.einsum("gqd,gkd->gqk", grad_wide, value_tiles)
        grad_scores = (weights * (grad_weights - row_dot) * scale).astype(jnp.bfloat16)
        grad_scores = lax.optimization_barrier(grad_scores).astype(jnp.float32)
        grad_query = jnp.einsum("gqk,gkd->gqd", grad_scores, key_tiles)
        key_terms = jnp.einsum("gqk,gqd->gkd", grad_scores, query_wide).reshape(-1, BLOCK, HEAD)
        value_terms = jnp.einsum("gqk,gqd->gkd", weights_low, grad_wide).reshape(-1, BLOCK, HEAD)
        key_total, value_total = totals
        return (key_total.at[flat_index].add(key_terms), value_total.at[flat_index].add(value_terms)), grad_query

    start = (jnp.zeros(key_source.shape, jnp.float32), jnp.zeros(key_source.shape, jnp.float32))
    totals, grad_query = lax.scan(step, start, (query_rows.reshape(count, 4, BLOCK, HEAD), grad_rows.reshape(count, 4, BLOCK, HEAD), tile_index.reshape(count, 4, -1)))
    return grad_query.reshape(pairs, BLOCK, HEAD), totals[0], totals[1]


def one_section(inputs):
    query_section, key_section, value_section, grad_section, global_section, random_section = inputs
    query_rows = query_section.reshape(SEQ_LEN, HEADS, HEAD).transpose(1, 0, 2).reshape(HEADS * NBLK, BLOCK, HEAD)
    grad_rows = grad_section.reshape(SEQ_LEN, HEADS, HEAD).transpose(1, 0, 2).reshape(HEADS * NBLK, BLOCK, HEAD)
    key_source = key_section.reshape(SEQ_LEN, KV_HEADS, HEAD).transpose(1, 0, 2).reshape(KV_HEADS * NBLK, BLOCK, HEAD)
    value_source = value_section.reshape(SEQ_LEN, KV_HEADS, HEAD).transpose(1, 0, 2).reshape(KV_HEADS * NBLK, BLOCK, HEAD)
    lists = block_lists(global_section, random_section, 0, NBLK)
    offset = (jnp.arange(HEADS, dtype=jnp.int32) // GROUP) * NBLK
    tile_index = (lists + offset[:, None, None]).reshape(HEADS * NBLK, -1)
    grad_query, key_total, value_total = backward_tiles(query_rows, grad_rows, key_source, value_source, tile_index)
    query_out = grad_query.astype(jnp.bfloat16).reshape(HEADS, SEQ_LEN, HEAD).transpose(1, 0, 2).reshape(SEQ_LEN, HEADS * HEAD)
    key_out = key_total.astype(jnp.bfloat16).reshape(KV_HEADS, SEQ_LEN, HEAD).transpose(1, 0, 2).reshape(SEQ_LEN, KV_HEADS * HEAD)
    value_out = value_total.astype(jnp.bfloat16).reshape(KV_HEADS, SEQ_LEN, HEAD).transpose(1, 0, 2).reshape(SEQ_LEN, KV_HEADS * HEAD)
    return query_out, key_out, value_out


def next_section(stacked):
    return jnp.concatenate([stacked[1:], jnp.zeros_like(stacked[:1])], axis=0)


def reference(queries, keys, values, out_grad, global_blocks, random_blocks):
    query_grad, key_grad, value_grad = lax.map(one_section, (queries, keys, values, out_grad, global_blocks, random_blocks))
    return query_grad, key_grad, value_grad, next_section(query_grad), next_section(key_grad), next_section(value_grad)
```

```python
import functools

import jax
import jax.numpy as jnp
from jax import lax
from jax.experimental import pallas as pl
from jax.experimental.pallas import tpu as pltpu
from jax.sharding import PartitionSpec as P

HEADS = 32
KV_HEADS = 4
HEAD = 128
BLOCK = 128
GROUP = HEADS // KV_HEADS
SCALE = HEAD ** -0.5
LOG2E = 1.4426950408889634

NT = (((1,), (1,)), ((), ()))
NN = (((1,), (0,)), ((), ()))


def attend(nblk, nloc, nglob, nrand, first_ref, glob_ref, rand_ref, q_ref, g_ref, k_ref, v_ref, dq_ref, dkv_ref, dk_acc, dv_acc, kt_ref):
    group = pl.program_id(0)
    first = first_ref[0]
    dk_acc[...] = jnp.zeros_like(dk_acc)
    dv_acc[...] = jnp.zeros_like(dv_acc)
    for b in range(nblk):
        rows = slice(b * BLOCK, (b + 1) * BLOCK)
        kt_ref[:, rows] = k_ref[rows, :].T

    def head(j, carry):
        h = group * GROUP + j
        cols = pl.ds(pl.multiple_of(j * HEAD, HEAD), HEAD)
        for b in range(nloc):
            at = first + b
            picks = [lax.rem(at + nblk - 1, nblk), at, lax.rem(at + 1, nblk)]
            picks += [glob_ref[h * nglob + n] for n in range(nglob)]
            picks += [rand_ref[(h * nblk + at) * nrand + n] for n in range(nrand)]
            spans = [pl.ds(pl.multiple_of(p * BLOCK, BLOCK), BLOCK) for p in picks]
            q = q_ref[b * BLOCK : (b + 1) * BLOCK, cols]
            g = g_ref[b * BLOCK : (b + 1) * BLOCK, cols]
            keys = jnp.concatenate([k_ref[s, :] for s in spans], axis=0)
            vals = jnp.concatenate([v_ref[s, :] for s in spans], axis=0)
            s = lax.dot_general(keys, q, NT, preferred_element_type=jnp.float32)
            top = jnp.max(s, axis=0, keepdims=True)
            p = jnp.exp2((s - top) * (SCALE * LOG2E))
            w = p * (1.0 / jnp.sum(p, axis=0, keepdims=True))
            low = w.astype(jnp.bfloat16)
            gw = lax.dot_general(vals, g, NT, preferred_element_type=jnp.float32)
            dot = jnp.sum(low.astype(jnp.float32) * gw, axis=0, keepdims=True)
            ds = (w * (gw - dot) * SCALE).astype(jnp.bfloat16)
            dk = lax.dot_general(ds, q, NN, preferred_element_type=jnp.float32)
            dv = lax.dot_general(low, g, NN, preferred_element_type=jnp.float32)
            kt = jnp.concatenate([kt_ref[:, s] for s in spans], axis=1)
            dqt = lax.dot_general(kt, ds, NN, preferred_element_type=jnp.float32)
            dq_ref[b * BLOCK : (b + 1) * BLOCK, cols] = dqt.T.astype(jnp.bfloat16)
            for n, span in enumerate(spans):
                dk_acc[span, :] += dk[n * BLOCK : (n + 1) * BLOCK, :]
                dv_acc[span, :] += dv[n * BLOCK : (n + 1) * BLOCK, :]
        return carry

    lax.fori_loop(0, GROUP, head, 0)
    dkv_ref[:, :HEAD] = dk_acc[...].astype(jnp.bfloat16)
    dkv_ref[:, HEAD:] = dv_acc[...].astype(jnp.bfloat16)


def local_backward(query, grad, kv, first, global_rows, random_rows):
    tokens = query.shape[0]
    seq = kv.shape[0]
    nblk = seq // BLOCK
    wide = GROUP * HEAD
    kernel = functools.partial(attend, nblk, tokens // BLOCK, global_rows.shape[-1], random_rows.shape[-1])
    smem = pl.BlockSpec(memory_space=pltpu.SMEM)
    return pl.pallas_call(
        kernel,
        grid=(KV_HEADS,),
        in_specs=[
            smem,
            smem,
            smem,
            pl.BlockSpec((tokens, wide), lambda g: (0, g)),
            pl.BlockSpec((tokens, wide), lambda g: (0, g)),
            pl.BlockSpec((seq, HEAD), lambda g: (0, g)),
            pl.BlockSpec((seq, HEAD), lambda g: (0, KV_HEADS + g)),
        ],
        out_specs=[
            pl.BlockSpec((tokens, wide), lambda g: (0, g)),
            pl.BlockSpec((seq, 2 * HEAD), lambda g: (0, g)),
        ],
        out_shape=[
            jax.ShapeDtypeStruct((tokens, HEADS * HEAD), jnp.bfloat16),
            jax.ShapeDtypeStruct((seq, 2 * KV_HEADS * HEAD), jnp.bfloat16),
        ],
        scratch_shapes=[
            pltpu.VMEM((seq, HEAD), jnp.float32),
            pltpu.VMEM((seq, HEAD), jnp.float32),
            pltpu.VMEM((HEAD, seq), jnp.bfloat16),
        ],
        compiler_params=pltpu.CompilerParams(vmem_limit_bytes=56 * 1024 * 1024),
        name="attend",
    )(first.reshape(1), global_rows.reshape(-1), random_rows.reshape(-1), query, grad, kv, kv)


def from_behind(value, axis):
    size = lax.axis_size(axis)
    return lax.ppermute(value, axis, [(i, i - 1) for i in range(1, size)])


def body(queries, keys, values, out_grad, global_blocks, random_blocks):
    tokens = queries.shape[1]
    device = lax.axis_index("seq")
    kv = jnp.concatenate([keys[0], values[0]], axis=1)
    kv = lax.all_gather(kv, "seq", axis=0, tiled=True)
    first = (device * (tokens // BLOCK)).astype(jnp.int32)
    query_grad, partial = local_backward(queries[0], out_grad[0], kv, first, global_blocks[0], random_blocks[0])
    incoming_query = from_behind(query_grad, "pipe")
    mine = lax.psum_scatter(partial, "seq", scatter_dimension=0, tiled=True)
    mine = mine.reshape(tokens, KV_HEADS, 2, HEAD)
    key_grad = mine[:, :, 0].reshape(tokens, KV_HEADS * HEAD)
    value_grad = mine[:, :, 1].reshape(tokens, KV_HEADS * HEAD)
    incoming_key, incoming_value = from_behind((key_grad, value_grad), "pipe")
    return tuple(x[None] for x in (query_grad, key_grad, value_grad, incoming_query, incoming_key, incoming_value))


def solution(mesh):
    part = P("pipe", "seq", None)
    in_specs = (part, part, part, part, P("pipe", None, None), P("pipe", None, None, None))
    return jax.shard_map(body, mesh=mesh, in_specs=in_specs, out_specs=(part,) * 6, check_vma=False)
```

```python
import functools

import jax
import jax.numpy as jnp
from jax import lax
from jax.experimental import pallas as pl
from jax.experimental.pallas import tpu as pltpu
from jax.sharding import PartitionSpec as P

HEADS = 32
KV_HEADS = 4
HEAD = 128
BLOCK = 128
GROUP = HEADS // KV_HEADS
SCALE = HEAD ** -0.5
LOG2E = 1.4426950408889634

NT = (((1,), (1,)), ((), ()))
NN = (((1,), (0,)), ((), ()))


def attend(nblk, nloc, nglob, nrand, first_ref, glob_ref, rand_ref, q_ref, g_ref, k_ref, v_ref, dq_ref, dkv_ref, dk_acc, dv_acc, kt_ref):
    group = pl.program_id(0)
    first = first_ref[0]
    dk_acc[...] = jnp.zeros_like(dk_acc)
    dv_acc[...] = jnp.zeros_like(dv_acc)
    for b in range(nblk):
        rows = slice(b * BLOCK, (b + 1) * BLOCK)
        kt_ref[:, rows] = k_ref[rows, :].T

    def head(j, carry):
        h = group * GROUP + j
        cols = pl.ds(pl.multiple_of(j * HEAD, HEAD), HEAD)
        for b in range(nloc):
            at = first + b
            picks = [lax.rem(at + nblk - 1, nblk), at, lax.rem(at + 1, nblk)]
            picks += [glob_ref[h * nglob + n] for n in range(nglob)]
            picks += [rand_ref[(h * nblk + at) * nrand + n] for n in range(nrand)]
            spans = [pl.ds(pl.multiple_of(p * BLOCK, BLOCK), BLOCK) for p in picks]
            q = q_ref[b * BLOCK : (b + 1) * BLOCK, cols]
            g = g_ref[b * BLOCK : (b + 1) * BLOCK, cols]
            keys = jnp.concatenate([k_ref[s, :] for s in spans], axis=0)
            vals = jnp.concatenate([v_ref[s, :] for s in spans], axis=0)
            s = lax.dot_general(keys, q, NT, preferred_element_type=jnp.float32)
            top = jnp.max(s, axis=0, keepdims=True)
            p = jnp.exp2((s - top) * (SCALE * LOG2E))
            w = p * (1.0 / jnp.sum(p, axis=0, keepdims=True))
            low = w.astype(jnp.bfloat16)
            gw = lax.dot_general(vals, g, NT, preferred_element_type=jnp.float32)
            dot = jnp.sum(low.astype(jnp.float32) * gw, axis=0, keepdims=True)
            ds = (w * (gw - dot) * SCALE).astype(jnp.bfloat16)
            dk = lax.dot_general(ds, q, NN, preferred_element_type=jnp.float32)
            dv = lax.dot_general(low, g, NN, preferred_element_type=jnp.float32)
            kt = jnp.concatenate([kt_ref[:, s] for s in spans], axis=1)
            dqt = lax.dot_general(kt, ds, NN, preferred_element_type=jnp.float32)
            dq_ref[b * BLOCK : (b + 1) * BLOCK, cols] = dqt.T.astype(jnp.bfloat16)
            for n, span in enumerate(spans):
                dk_acc[span, :] += dk[n * BLOCK : (n + 1) * BLOCK, :]
                dv_acc[span, :] += dv[n * BLOCK : (n + 1) * BLOCK, :]
        return carry

    lax.fori_loop(0, GROUP, head, 0)
    dkv_ref[:, :HEAD] = dk_acc[...].astype(jnp.bfloat16)
    dkv_ref[:, HEAD:] = dv_acc[...].astype(jnp.bfloat16)


def local_backward(query, grad, k_all, v_all, first, global_rows, random_rows):
    tokens = query.shape[0]
    seq = k_all.shape[0]
    nblk = seq // BLOCK
    wide = GROUP * HEAD
    kernel = functools.partial(attend, nblk, tokens // BLOCK, global_rows.shape[-1], random_rows.shape[-1])
    smem = pl.BlockSpec(memory_space=pltpu.SMEM)
    return pl.pallas_call(
        kernel,
        grid=(KV_HEADS,),
        in_specs=[
            smem,
            smem,
            smem,
            pl.BlockSpec((tokens, wide), lambda g: (0, g)),
            pl.BlockSpec((tokens, wide), lambda g: (0, g)),
            pl.BlockSpec((seq, HEAD), lambda g: (0, g)),
            pl.BlockSpec((seq, HEAD), lambda g: (0, g)),
        ],
        out_specs=[
            pl.BlockSpec((tokens, wide), lambda g: (0, g)),
            pl.BlockSpec((seq, 2 * HEAD), lambda g: (0, g)),
        ],
        out_shape=[
            jax.ShapeDtypeStruct((tokens, HEADS * HEAD), jnp.bfloat16),
            jax.ShapeDtypeStruct((seq, 2 * KV_HEADS * HEAD), jnp.bfloat16),
        ],
        scratch_shapes=[
            pltpu.VMEM((seq, HEAD), jnp.float32),
            pltpu.VMEM((seq, HEAD), jnp.float32),
            pltpu.VMEM((HEAD, seq), jnp.bfloat16),
        ],
        compiler_params=pltpu.CompilerParams(vmem_limit_bytes=56 * 1024 * 1024),
        name="attend",
    )(first.reshape(1), global_rows.reshape(-1), random_rows.reshape(-1), query, grad, k_all, v_all)


def ring_place():
    me = lax.axis_index("seq")
    z = me // 2
    x = me % 2
    return me, z, x


def greet(edges):
    barrier = pltpu.get_barrier_semaphore()
    for there, to in edges:
        @pl.when(there)
        def _(to=to):
            pl.semaphore_signal(barrier, inc=1, device_id=to, device_id_type=pl.DeviceIdType.MESH)
    pl.semaphore_wait(barrier, sum(jnp.where(there, 1, 0) for there, _ in edges))


def gather_kernel(n, k_ref, v_ref, ko_ref, vo_ref, own_sem, send_sem, recv_sem):
    levels = n // 2
    me, z, x = ring_place()
    partner, up, down = me + 1 - 2 * x, me + 2, me - 2
    tokens = k_ref.shape[0]
    sources, outs = (k_ref, v_ref), (ko_ref, vo_ref)
    greet([(z >= 0, {"seq": partner}), (z < levels - 1, {"seq": up}), (z > 0, {"seq": down})])

    def place(i, shard):
        return outs[i].at[pl.ds(pl.multiple_of(shard * tokens, tokens), tokens), :]

    def copy(i, shard, way, to, src=None):
        spot = place(i, shard)
        return pltpu.make_async_remote_copy(
            src_ref=spot if src is None else src,
            dst_ref=spot,
            send_sem=send_sem.at[way, i, shard],
            recv_sem=recv_sem.at[i, shard],
            device_id={"seq": to},
            device_id_type=pl.DeviceIdType.MESH,
        )

    owns = [pltpu.make_async_copy(sources[i], place(i, me), own_sem.at[i]) for i in range(2)]
    for i in range(2):
        @pl.when(z < levels - 1)
        def _(i=i):
            copy(i, me, 0, up, sources[i]).start()

        @pl.when(z > 0)
        def _(i=i):
            copy(i, me, 1, down, sources[i]).start()

        copy(i, me, 2, partner, sources[i]).start()
    for own in owns:
        own.start()
    for t in range(1, levels):
        for i in range(2):
            @pl.when(z >= t)
            def _(i=i, t=t):
                shard = me - 2 * t
                copy(i, shard, 2, partner).wait_recv()

                @pl.when(z < levels - 1)
                def _():
                    copy(i, shard, 0, up).start()

                copy(i, shard, 2, partner).start()

            @pl.when(z + t < levels)
            def _(i=i, t=t):
                shard = me + 2 * t
                copy(i, shard, 2, partner).wait_recv()

                @pl.when(z > 0)
                def _():
                    copy(i, shard, 1, down).start()

                copy(i, shard, 2, partner).start()
    for i in range(2):
        for level in range(levels):
            copy(i, 2 * level + 1 - x, 2, partner).wait_recv()
            copy(i, 2 * level + x, 2, partner).wait_send()

            @pl.when((level <= z) & (z < levels - 1))
            def _(i=i, level=level):
                copy(i, 2 * level + x, 0, up).wait_send()

            @pl.when((level >= z) & (z > 0))
            def _(i=i, level=level):
                copy(i, 2 * level + x, 1, down).wait_send()
    for own in owns:
        own.wait()


def gather_rows(keys, values):
    n = lax.axis_size("seq")
    tokens, width = keys.shape
    whole = jax.ShapeDtypeStruct((n * tokens, width), keys.dtype)
    hbm = pl.BlockSpec(memory_space=pl.ANY)
    return pl.pallas_call(
        functools.partial(gather_kernel, n),
        in_specs=[hbm, hbm],
        out_specs=[hbm, hbm],
        out_shape=[whole, whole],
        scratch_shapes=[
            pltpu.SemaphoreType.DMA((2,)),
            pltpu.SemaphoreType.DMA((3, 2, n)),
            pltpu.SemaphoreType.DMA((2, n)),
        ],
        compiler_params=pltpu.CompilerParams(collective_id=0, has_side_effects=True),
        name="gather_rows",
    )(keys, values)


PIECES = 2


def reduce_kernel(n, sections, part_ref, dk_ref, dv_ref, ik_ref, iv_ref, xbuf, ubuf, dbuf, xs, xr, us, ur, ds, dr, ps, pr):
    levels = n // 2
    me, z, x = ring_place()
    section = lax.axis_index("pipe")
    partner, up, down = me + 1 - 2 * x, me + 2, me - 2
    tokens = dk_ref.shape[0]
    rows = tokens // PIECES
    greet([
        (z >= 0, {"seq": partner}),
        (z < levels - 1, {"seq": up}),
        (z > 0, {"seq": down}),
        (section > 0, {"pipe": section - 1}),
        (section < sections - 1, {"pipe": section + 1}),
    ])

    def at(ref, level, k):
        return ref.at[pl.ds(pl.multiple_of(level * tokens + k * rows, rows), rows), :]

    def remote(src, dst, send, recv, to):
        return pltpu.make_async_remote_copy(
            src_ref=src, dst_ref=dst, send_sem=send, recv_sem=recv,
            device_id=to, device_id_type=pl.DeviceIdType.MESH,
        )

    def across(level, k):
        return remote(at(part_ref, 2 * level + 1 - x, k), at(xbuf, level, k), xs.at[level, k], xr.at[level, k], {"seq": partner})

    def upward(level, k):
        return remote(at(xbuf, level, k), at(ubuf, level, k), us.at[level, k], ur.at[level, k], {"seq": up})

    def downward(level, k):
        return remote(at(xbuf, level, k), at(dbuf, level, k), ds.at[level, k], dr.at[level, k], {"seq": down})

    def each_far(action):
        for t in range(levels - 1, 0, -1):
            for k in range(PIECES):
                @pl.when(z + t < levels)
                def _(t=t, k=k):
                    action(z + t, k, True)

                @pl.when(z >= t)
                def _(t=t, k=k):
                    action(z - t, k, False)

    each_far(lambda level, k, rising: across(level, k).start())
    for k in range(PIECES):
        across(z, k).start()

    def load(ref, level, k):
        return ref[pl.ds(pl.multiple_of(level * tokens + k * rows, rows), rows), :]

    def add(level, k, value):
        spot = pl.ds(pl.multiple_of(level * tokens + k * rows, rows), rows)
        xbuf[spot, :] = (xbuf[spot, :].astype(jnp.float32) + value.astype(jnp.float32)).astype(jnp.bfloat16)

    def pass_on(level, k, rising):
        across(level, k).wait_recv()
        mine = load(part_ref, 2 * level + x, k).astype(jnp.float32)
        if rising:
            @pl.when(z > 0)
            def _():
                upward(level, k).wait_recv()
                add(level, k, mine + load(ubuf, level, k).astype(jnp.float32))

            @pl.when(z == 0)
            def _():
                add(level, k, mine)

            upward(level, k).start()
        else:
            @pl.when(z < levels - 1)
            def _():
                downward(level, k).wait_recv()
                add(level, k, mine + load(dbuf, level, k).astype(jnp.float32))

            @pl.when(z == levels - 1)
            def _():
                add(level, k, mine)

            downward(level, k).start()

    each_far(pass_on)

    def shift(src, dst, i, k):
        spot = pl.ds(k * rows, rows)
        return remote(src.at[spot, :], dst.at[spot, :], ps.at[i, k], pr.at[i, k], {"pipe": section - 1})

    pairs = ((dk_ref, ik_ref), (dv_ref, iv_ref))
    for k in range(PIECES):
        across(z, k).wait_recv()

        @pl.when(z > 0)
        def _(k=k):
            upward(z, k).wait_recv()

        @pl.when(z < levels - 1)
        def _(k=k):
            downward(z, k).wait_recv()

        below = jnp.where(z > 0, load(ubuf, z, k).astype(jnp.float32), 0.0)
        above = jnp.where(z < levels - 1, load(dbuf, z, k).astype(jnp.float32), 0.0)
        total = load(part_ref, me, k).astype(jnp.float32) + load(xbuf, z, k).astype(jnp.float32)
        total = (total + below + above).astype(jnp.bfloat16)
        spot = slice(k * rows, (k + 1) * rows)
        for g in range(KV_HEADS):
            cols = slice(g * HEAD, (g + 1) * HEAD)
            dk_ref[spot, cols] = total[:, 2 * g * HEAD : (2 * g + 1) * HEAD]
            dv_ref[spot, cols] = total[:, (2 * g + 1) * HEAD : (2 * g + 2) * HEAD]

        @pl.when(section > 0)
        def _(k=k):
            for i, (src, dst) in enumerate(pairs):
                shift(src, dst, i, k).start()

    @pl.when(section == sections - 1)
    def _():
        ik_ref[...] = jnp.zeros_like(ik_ref)
        iv_ref[...] = jnp.zeros_like(iv_ref)

    each_far(lambda level, k, rising: (across(level, k).wait_send(), (upward if rising else downward)(level, k).wait_send()))
    for k in range(PIECES):
        across(z, k).wait_send()
        for i, (src, dst) in enumerate(pairs):
            @pl.when(section < sections - 1)
            def _(i=i, k=k, src=src, dst=dst):
                shift(src, dst, i, k).wait_recv()

            @pl.when(section > 0)
            def _(i=i, k=k, src=src, dst=dst):
                shift(src, dst, i, k).wait_send()


def reduce_rows(partial):
    n = lax.axis_size("seq")
    tokens = partial.shape[0] // n
    wide = partial.shape[1]
    half = jax.ShapeDtypeStruct((tokens, wide // 2), partial.dtype)
    vmem = pl.BlockSpec(memory_space=pltpu.VMEM)
    slots = pltpu.VMEM((n // 2 * tokens, wide), partial.dtype)
    dma = pltpu.SemaphoreType.DMA((n // 2, PIECES))
    return pl.pallas_call(
        functools.partial(reduce_kernel, n, lax.axis_size("pipe")),
        in_specs=[vmem],
        out_specs=[vmem] * 4,
        out_shape=[half] * 4,
        scratch_shapes=[slots] * 3 + [dma] * 6 + [pltpu.SemaphoreType.DMA((2, PIECES))] * 2,
        compiler_params=pltpu.CompilerParams(
            collective_id=1, has_side_effects=True, vmem_limit_bytes=58 * 1024 * 1024
        ),
        name="reduce_rows",
    )(partial)


def from_behind(value, axis):
    size = lax.axis_size(axis)
    return lax.ppermute(value, axis, [(i, i - 1) for i in range(1, size)])


def body(queries, keys, values, out_grad, global_blocks, random_blocks):
    tokens = queries.shape[1]
    device = lax.axis_index("seq")
    k_all, v_all = gather_rows(keys[0], values[0])
    first = (device * (tokens // BLOCK)).astype(jnp.int32)
    query_grad, partial = local_backward(queries[0], out_grad[0], k_all, v_all, first, global_blocks[0], random_blocks[0])
    incoming_query = from_behind(query_grad, "pipe")
    key_grad, value_grad, incoming_key, incoming_value = reduce_rows(partial)
    return tuple(x[None] for x in (query_grad, key_grad, value_grad, incoming_query, incoming_key, incoming_value))


def solution(mesh):
    part = P("pipe", "seq", None)
    in_specs = (part, part, part, part, P("pipe", None, None), P("pipe", None, None, None))
    return jax.shard_map(body, mesh=mesh, in_specs=in_specs, out_specs=(part,) * 6, check_vma=False)
```

```python
import functools

import jax
import jax.numpy as jnp
from jax import lax
from jax.experimental import pallas as pl
from jax.experimental.pallas import tpu as pltpu
from jax.sharding import PartitionSpec as P

HEADS = 32
KV_HEADS = 4
HEAD = 128
BLOCK = 128
GROUP = HEADS // KV_HEADS
SCALE = HEAD ** -0.5
LOG2E = 1.4426950408889634

NT = (((1,), (1,)), ((), ()))
NN = (((1,), (0,)), ((), ()))


def attend(nblk, nloc, nglob, nrand, first_ref, glob_ref, rand_ref, q_ref, g_ref, k_ref, v_ref, dq_ref, dkv_ref, dk_acc, dv_acc, kt_ref):
    group = pl.program_id(0)
    first = first_ref[0]
    dk_acc[...] = jnp.zeros_like(dk_acc)
    dv_acc[...] = jnp.zeros_like(dv_acc)
    for b in range(nblk):
        rows = slice(b * BLOCK, (b + 1) * BLOCK)
        kt_ref[:, rows] = k_ref[rows, :].T

    def listed(h, b):
        at = first + b
        picks = [lax.rem(at + nblk - 1, nblk), at, lax.rem(at + 1, nblk)]
        picks += [glob_ref[h * nglob + n] for n in range(nglob)]
        picks += [rand_ref[(h * nblk + at) * nrand + n] for n in range(nrand)]
        return [pl.ds(pl.multiple_of(p * BLOCK, BLOCK), BLOCK) for p in picks]

    def products(spans, rows, cols):
        q, g = q_ref[rows, cols], g_ref[rows, cols]
        keys = jnp.concatenate([k_ref[s, :] for s in spans], axis=0)
        vals = jnp.concatenate([v_ref[s, :] for s in spans], axis=0)
        s = lax.dot_general(keys, q, NT, preferred_element_type=jnp.float32)
        gw = lax.dot_general(vals, g, NT, preferred_element_type=jnp.float32)
        cut = lambda x: [x[n * BLOCK : (n + 1) * BLOCK, :] for n in range(len(spans))]
        return cut(s), cut(gw)

    def gradients(spans, rows, cols, s, gw):
        q, g = q_ref[rows, cols], g_ref[rows, cols]
        count = len(spans)
        top = functools.reduce(jnp.maximum, [jnp.max(x, axis=0, keepdims=True) for x in s])
        p, total, mixed = [], 0.0, 0.0
        for x, y in zip(s, gw):
            e = jnp.exp2((x - top) * (SCALE * LOG2E))
            p.append(e)
            total = total + jnp.sum(e, axis=0, keepdims=True)
            mixed = mixed + jnp.sum(e * y, axis=0, keepdims=True)
        inv = 1.0 / total
        dot = mixed * inv
        inv_scaled = inv * SCALE
        low = jnp.concatenate([(x * inv).astype(jnp.bfloat16) for x in p], axis=0)
        ds = jnp.concatenate(
            [((x * inv_scaled) * (y - dot)).astype(jnp.bfloat16) for x, y in zip(p, gw)], axis=0
        )
        dv = lax.dot_general(low, g, NN, preferred_element_type=jnp.float32)
        dk = lax.dot_general(ds, q, NN, preferred_element_type=jnp.float32)
        kt = jnp.concatenate([kt_ref[:, s] for s in spans], axis=1)
        dqt = lax.dot_general(kt, ds, NN, preferred_element_type=jnp.float32)
        dq_ref[rows, cols] = dqt.T.astype(jnp.bfloat16)
        for n, span in enumerate(spans):
            dk_acc[span, :] += dk[n * BLOCK : (n + 1) * BLOCK, :]
            dv_acc[span, :] += dv[n * BLOCK : (n + 1) * BLOCK, :]

    def head(j, carry):
        h = group * GROUP + j
        cols = pl.ds(pl.multiple_of(j * HEAD, HEAD), HEAD)
        work = [(listed(h, b), slice(b * BLOCK, (b + 1) * BLOCK), cols) for b in range(nloc)]
        made = [products(*w) for w in work]
        for w, m in zip(work, made):
            gradients(*w, *m)
        return carry

    lax.fori_loop(0, GROUP, head, 0, unroll=2)
    dkv_ref[:, :HEAD] = dk_acc[...].astype(jnp.bfloat16)
    dkv_ref[:, HEAD:] = dv_acc[...].astype(jnp.bfloat16)


def local_backward(query, grad, k_all, v_all, first, global_rows, random_rows):
    tokens = query.shape[0]
    seq = k_all.shape[0]
    nblk = seq // BLOCK
    wide = GROUP * HEAD
    kernel = functools.partial(attend, nblk, tokens // BLOCK, global_rows.shape[-1], random_rows.shape[-1])
    smem = pl.BlockSpec(memory_space=pltpu.SMEM)
    return pl.pallas_call(
        kernel,
        grid=(KV_HEADS,),
        in_specs=[
            smem,
            smem,
            smem,
            pl.BlockSpec((tokens, wide), lambda g: (0, g)),
            pl.BlockSpec((tokens, wide), lambda g: (0, g)),
            pl.BlockSpec((seq, HEAD), lambda g: (0, g)),
            pl.BlockSpec((seq, HEAD), lambda g: (0, g)),
        ],
        out_specs=[
            pl.BlockSpec((tokens, wide), lambda g: (0, g)),
            pl.BlockSpec((seq, 2 * HEAD), lambda g: (0, g)),
        ],
        out_shape=[
            jax.ShapeDtypeStruct((tokens, HEADS * HEAD), jnp.bfloat16),
            jax.ShapeDtypeStruct((seq, 2 * KV_HEADS * HEAD), jnp.bfloat16),
        ],
        scratch_shapes=[
            pltpu.VMEM((seq, HEAD), jnp.float32),
            pltpu.VMEM((seq, HEAD), jnp.float32),
            pltpu.VMEM((HEAD, seq), jnp.bfloat16),
        ],
        compiler_params=pltpu.CompilerParams(vmem_limit_bytes=56 * 1024 * 1024),
        name="attend",
    )(first.reshape(1), global_rows.reshape(-1), random_rows.reshape(-1), query, grad, k_all, v_all)


def ring_place():
    me = lax.axis_index("seq")
    z = me // 2
    x = me % 2
    return me, z, x


def greet(edges):
    barrier = pltpu.get_barrier_semaphore()
    for there, to in edges:
        @pl.when(there)
        def _(to=to):
            pl.semaphore_signal(barrier, inc=1, device_id=to, device_id_type=pl.DeviceIdType.MESH)
    pl.semaphore_wait(barrier, sum(jnp.where(there, 1, 0) for there, _ in edges))


def gather_kernel(n, k_ref, v_ref, ko_ref, vo_ref, own_sem, send_sem, recv_sem):
    levels = n // 2
    me, z, x = ring_place()
    partner, up, down = me + 1 - 2 * x, me + 2, me - 2
    tokens = k_ref.shape[0]
    sources, outs = (k_ref, v_ref), (ko_ref, vo_ref)
    greet([(z >= 0, {"seq": partner}), (z < levels - 1, {"seq": up}), (z > 0, {"seq": down})])

    def place(i, shard):
        return outs[i].at[pl.ds(pl.multiple_of(shard * tokens, tokens), tokens), :]

    def copy(i, shard, way, to, src=None):
        spot = place(i, shard)
        return pltpu.make_async_remote_copy(
            src_ref=spot if src is None else src,
            dst_ref=spot,
            send_sem=send_sem.at[way, i, shard],
            recv_sem=recv_sem.at[i, shard],
            device_id={"seq": to},
            device_id_type=pl.DeviceIdType.MESH,
        )

    owns = [pltpu.make_async_copy(sources[i], place(i, me), own_sem.at[i]) for i in range(2)]
    for i in range(2):
        @pl.when(z < levels - 1)
        def _(i=i):
            copy(i, me, 0, up, sources[i]).start()

        @pl.when(z > 0)
        def _(i=i):
            copy(i, me, 1, down, sources[i]).start()

        copy(i, me, 2, partner, sources[i]).start()
    for own in owns:
        own.start()
    for t in range(1, levels):
        for i in range(2):
            @pl.when(z >= t)
            def _(i=i, t=t):
                shard = me - 2 * t
                copy(i, shard, 2, partner).wait_recv()

                @pl.when(z < levels - 1)
                def _():
                    copy(i, shard, 0, up).start()

                copy(i, shard, 2, partner).start()

            @pl.when(z + t < levels)
            def _(i=i, t=t):
                shard = me + 2 * t
                copy(i, shard, 2, partner).wait_recv()

                @pl.when(z > 0)
                def _():
                    copy(i, shard, 1, down).start()

                copy(i, shard, 2, partner).start()
    for i in range(2):
        for level in range(levels):
            copy(i, 2 * level + 1 - x, 2, partner).wait_recv()
            copy(i, 2 * level + x, 2, partner).wait_send()

            @pl.when((level <= z) & (z < levels - 1))
            def _(i=i, level=level):
                copy(i, 2 * level + x, 0, up).wait_send()

            @pl.when((level >= z) & (z > 0))
            def _(i=i, level=level):
                copy(i, 2 * level + x, 1, down).wait_send()
    for own in owns:
        own.wait()


def gather_rows(keys, values):
    n = lax.axis_size("seq")
    tokens, width = keys.shape
    whole = jax.ShapeDtypeStruct((n * tokens, width), keys.dtype)
    hbm = pl.BlockSpec(memory_space=pl.ANY)
    return pl.pallas_call(
        functools.partial(gather_kernel, n),
        in_specs=[hbm, hbm],
        out_specs=[hbm, hbm],
        out_shape=[whole, whole],
        scratch_shapes=[
            pltpu.SemaphoreType.DMA((2,)),
            pltpu.SemaphoreType.DMA((3, 2, n)),
            pltpu.SemaphoreType.DMA((2, n)),
        ],
        compiler_params=pltpu.CompilerParams(collective_id=0, has_side_effects=True),
        name="gather_rows",
    )(keys, values)


PIECES = 2


def reduce_kernel(n, sections, part_ref, dk_ref, dv_ref, ik_ref, iv_ref, xbuf, ubuf, dbuf, xs, xr, us, ur, ds, dr, ps, pr):
    levels = n // 2
    me, z, x = ring_place()
    section = lax.axis_index("pipe")
    partner, up, down = me + 1 - 2 * x, me + 2, me - 2
    tokens = dk_ref.shape[0]
    rows = tokens // PIECES
    greet([
        (z >= 0, {"seq": partner}),
        (z < levels - 1, {"seq": up}),
        (z > 0, {"seq": down}),
        (section > 0, {"pipe": section - 1}),
        (section < sections - 1, {"pipe": section + 1}),
    ])

    def at(ref, level, k):
        return ref.at[pl.ds(pl.multiple_of(level * tokens + k * rows, rows), rows), :]

    def remote(src, dst, send, recv, to):
        return pltpu.make_async_remote_copy(
            src_ref=src, dst_ref=dst, send_sem=send, recv_sem=recv,
            device_id=to, device_id_type=pl.DeviceIdType.MESH,
        )

    def across(level, k):
        return remote(at(part_ref, 2 * level + 1 - x, k), at(xbuf, level, k), xs.at[level, k], xr.at[level, k], {"seq": partner})

    def upward(level, k):
        return remote(at(xbuf, level, k), at(ubuf, level, k), us.at[level, k], ur.at[level, k], {"seq": up})

    def downward(level, k):
        return remote(at(xbuf, level, k), at(dbuf, level, k), ds.at[level, k], dr.at[level, k], {"seq": down})

    def each_far(action):
        for t in range(levels - 1, 0, -1):
            for k in range(PIECES):
                @pl.when(z + t < levels)
                def _(t=t, k=k):
                    action(z + t, k, True)

                @pl.when(z >= t)
                def _(t=t, k=k):
                    action(z - t, k, False)

    each_far(lambda level, k, rising: across(level, k).start())
    for k in range(PIECES):
        across(z, k).start()

    def load(ref, level, k):
        return ref[pl.ds(pl.multiple_of(level * tokens + k * rows, rows), rows), :]

    def add(level, k, value):
        spot = pl.ds(pl.multiple_of(level * tokens + k * rows, rows), rows)
        xbuf[spot, :] = (xbuf[spot, :].astype(jnp.float32) + value.astype(jnp.float32)).astype(jnp.bfloat16)

    def pass_on(level, k, rising):
        across(level, k).wait_recv()
        mine = load(part_ref, 2 * level + x, k).astype(jnp.float32)
        if rising:
            @pl.when(z > 0)
            def _():
                upward(level, k).wait_recv()
                add(level, k, mine + load(ubuf, level, k).astype(jnp.float32))

            @pl.when(z == 0)
            def _():
                add(level, k, mine)

            upward(level, k).start()
        else:
            @pl.when(z < levels - 1)
            def _():
                downward(level, k).wait_recv()
                add(level, k, mine + load(dbuf, level, k).astype(jnp.float32))

            @pl.when(z == levels - 1)
            def _():
                add(level, k, mine)

            downward(level, k).start()

    each_far(pass_on)

    def shift(src, dst, i, k):
        spot = pl.ds(k * rows, rows)
        return remote(src.at[spot, :], dst.at[spot, :], ps.at[i, k], pr.at[i, k], {"pipe": section - 1})

    pairs = ((dk_ref, ik_ref), (dv_ref, iv_ref))
    for k in range(PIECES):
        across(z, k).wait_recv()

        @pl.when(z > 0)
        def _(k=k):
            upward(z, k).wait_recv()

        @pl.when(z < levels - 1)
        def _(k=k):
            downward(z, k).wait_recv()

        below = jnp.where(z > 0, load(ubuf, z, k).astype(jnp.float32), 0.0)
        above = jnp.where(z < levels - 1, load(dbuf, z, k).astype(jnp.float32), 0.0)
        total = load(part_ref, me, k).astype(jnp.float32) + load(xbuf, z, k).astype(jnp.float32)
        total = (total + below + above).astype(jnp.bfloat16)
        spot = slice(k * rows, (k + 1) * rows)
        for g in range(KV_HEADS):
            cols = slice(g * HEAD, (g + 1) * HEAD)
            dk_ref[spot, cols] = total[:, 2 * g * HEAD : (2 * g + 1) * HEAD]
            dv_ref[spot, cols] = total[:, (2 * g + 1) * HEAD : (2 * g + 2) * HEAD]

        @pl.when(section > 0)
        def _(k=k):
            for i, (src, dst) in enumerate(pairs):
                shift(src, dst, i, k).start()

    @pl.when(section == sections - 1)
    def _():
        ik_ref[...] = jnp.zeros_like(ik_ref)
        iv_ref[...] = jnp.zeros_like(iv_ref)

    each_far(lambda level, k, rising: (across(level, k).wait_send(), (upward if rising else downward)(level, k).wait_send()))
    for k in range(PIECES):
        across(z, k).wait_send()
        for i, (src, dst) in enumerate(pairs):
            @pl.when(section < sections - 1)
            def _(i=i, k=k, src=src, dst=dst):
                shift(src, dst, i, k).wait_recv()

            @pl.when(section > 0)
            def _(i=i, k=k, src=src, dst=dst):
                shift(src, dst, i, k).wait_send()


def reduce_rows(partial):
    n = lax.axis_size("seq")
    tokens = partial.shape[0] // n
    wide = partial.shape[1]
    half = jax.ShapeDtypeStruct((tokens, wide // 2), partial.dtype)
    vmem = pl.BlockSpec(memory_space=pltpu.VMEM)
    slots = pltpu.VMEM((n // 2 * tokens, wide), partial.dtype)
    dma = pltpu.SemaphoreType.DMA((n // 2, PIECES))
    return pl.pallas_call(
        functools.partial(reduce_kernel, n, lax.axis_size("pipe")),
        in_specs=[vmem],
        out_specs=[vmem] * 4,
        out_shape=[half] * 4,
        scratch_shapes=[slots] * 3 + [dma] * 6 + [pltpu.SemaphoreType.DMA((2, PIECES))] * 2,
        compiler_params=pltpu.CompilerParams(
            collective_id=1, has_side_effects=True, vmem_limit_bytes=58 * 1024 * 1024
        ),
        name="reduce_rows",
    )(partial)


def from_behind(value, axis):
    size = lax.axis_size(axis)
    return lax.ppermute(value, axis, [(i, i - 1) for i in range(1, size)])


def body(queries, keys, values, out_grad, global_blocks, random_blocks):
    tokens = queries.shape[1]
    device = lax.axis_index("seq")
    k_all, v_all = gather_rows(keys[0], values[0])
    first = (device * (tokens // BLOCK)).astype(jnp.int32)
    query_grad, partial = local_backward(queries[0], out_grad[0], k_all, v_all, first, global_blocks[0], random_blocks[0])
    incoming_query = from_behind(query_grad, "pipe")
    key_grad, value_grad, incoming_key, incoming_value = reduce_rows(partial)
    return tuple(x[None] for x in (query_grad, key_grad, value_grad, incoming_query, incoming_key, incoming_value))


def solution(mesh):
    part = P("pipe", "seq", None)
    in_specs = (part, part, part, part, P("pipe", None, None), P("pipe", None, None, None))
    return jax.shard_map(body, mesh=mesh, in_specs=in_specs, out_specs=(part,) * 6, check_vma=False)
```
